32 devices in a mesh: gx: 2 (over y), gy: 4 (over z), gz: 4 (over x, core).
Axes of the slice: x: 2, y: 2, z: 4, core: 2. Of those that a mesh axis runs over, the one named last changes fastest.
Arguments:
- tokens: bfloat16 [256, 8192], P('gx', 'gz'), may hold values from -6 to 6
- gate_weight: bfloat16 [8192, 14336], P('gz', ('gx', 'gy')), may hold values from -0.0625 to 0.0625
- up_weight: bfloat16 [8192, 14336], P('gz', ('gx', 'gy')), may hold values from -0.0625 to 0.0625
- down_weight: bfloat16 [14336, 8192], P(('gx', 'gy'), 'gz'), may hold values from -0.046875 to 0.046875
- out_grad: bfloat16 [256, 8192], P('gx', 'gz'), may hold values from -6 to 6
Outputs:
- output: bfloat16 [256, 8192], P('gx', 'gz')
- input_grad: bfloat16 [256, 8192], P('gx', 'gz')
- gate_grad: bfloat16 [8192, 14336], P('gz', ('gx', 'gy'))
- up_grad: bfloat16 [8192, 14336], P('gz', ('gx', 'gy'))
- down_grad: bfloat16 [14336, 8192], P(('gx', 'gy'), 'gz')
The draws below stay inside these ranges and needn't reach their ends.
All inputs are finite; a program needn't handle non-finite values.
Results may differ from the reference program's by a relative error of at most 0.025.
Values may be sent and summed in bfloat16 or wider, within the bound.
A program may use at most 128 MiB of HBM per device.

```python
import jax
import jax.numpy as jnp
from jax import lax

D = 8192
FF = 14336
TOKENS = 256
N_GX = 2
N_GY = 4
N_GZ = 4


def block_scale(rng, extent, pieces, least, largest):
    factor_of = 1.0
    for axis_at, parts in pieces:
        steps = jax.random.uniform(jax.random.fold_in(jax.random.fold_in(rng, 6), axis_at), (parts,), jnp.float32, least / len(pieces), largest / len(pieces))
        factor_of = factor_of * jnp.repeat(jnp.exp(steps), extent[axis_at] // parts).reshape((-1,) + (1,) * (len(extent) - 1 - axis_at))
    return factor_of


def scatter_about(key, shape, scale, bound, pieces=(), kind=jnp.bfloat16):
    drawn = jax.random.normal(key, shape, jnp.float32) * scale
    if len(pieces) > 0:
        drawn = block_scale(key, shape, pieces, -0.22, 0.18) * drawn
    return jnp.clip(drawn, min=-bound, max=bound).astype(kind)


def setup_inputs(seed: int = 0) -> dict:
    key_of = jax.random.split(jax.random.key(seed), 6)
    return {
        "tokens": scatter_about(key_of[0], (TOKENS, D), 1.0, 6.0, ((0, 2), (1, 4))),
        "gate_weight": scatter_about(key_of[1], (D, FF), D ** -0.5, 0.0625, ((0, 4), (1, 8))),
        "up_weight": scatter_about(key_of[2], (D, FF), D ** -0.5, 0.0625, ((0, 4), (1, 8))),
        "down_weight": scatter_about(key_of[3], (FF, D), FF ** -0.5, 0.046875, ((0, 8), (1, 4))),
        "out_grad": scatter_about(key_of[4], (TOKENS, D), 1.0, 6.0, ((0, 2), (1, 4))),
    }


def contract_rows(left, right):
    return lax.dot_general(left, right, (((0,), (0,)), ((), ())), preferred_element_type=jnp.float32)


def contract_cols(left, right):
    return lax.dot_general(left, right, (((1,), (1,)), ((), ())), preferred_element_type=jnp.float32)


def reference(tokens, gate_weight, up_weight, down_weight, out_grad):
    feature_width = D // N_GZ

    def gate_block(carry, block_index):
        offset = (block_index * feature_width).astype(jnp.int32)
        rows = lax.dynamic_slice_in_dim(tokens, offset, feature_width, 1)
        gate_rows = lax.dynamic_slice_in_dim(gate_weight, offset, feature_width, 0)
        up_rows = lax.dynamic_slice_in_dim(up_weight, offset, feature_width, 0)
        gate_term = jnp.dot(rows, gate_rows, preferred_element_type=jnp.float32)
        up_term = jnp.dot(rows, up_rows, preferred_element_type=jnp.float32)
        gate_term = lax.optimization_barrier(gate_term.astype(jnp.bfloat16)).astype(jnp.float32)
        up_term = lax.optimization_barrier(up_term.astype(jnp.bfloat16)).astype(jnp.float32)
        return (carry[0] + gate_term, carry[1] + up_term), None

    empty = jnp.zeros((tokens.shape[0], FF), jnp.float32)
    (gate, upward), _ = lax.scan(gate_block, (empty, empty), jnp.arange(N_GZ, dtype=jnp.int32))
    sigmoid = jax.nn.sigmoid(gate)
    hidden = (gate * sigmoid * upward).astype(jnp.bfloat16)
    output = jnp.dot(hidden, down_weight, preferred_element_type=jnp.float32).astype(jnp.bfloat16)
    dhidden = contract_cols(out_grad, down_weight)
    dgate = (dhidden * upward * sigmoid * (1.0 + gate * (1.0 - sigmoid))).astype(jnp.bfloat16)
    dupward = (dhidden * gate * sigmoid).astype(jnp.bfloat16)
    hidden_width = FF // (N_GX * N_GY)

    def input_block(carry, block_index):
        offset = (block_index * hidden_width).astype(jnp.int32)
        grad_gate = lax.dynamic_slice_in_dim(dgate, offset, hidden_width, 1)
        grad_up = lax.dynamic_slice_in_dim(dupward, offset, hidden_width, 1)
        gate_cols = lax.dynamic_slice_in_dim(gate_weight, offset, hidden_width, 1)
        up_cols = lax.dynamic_slice_in_dim(up_weight, offset, hidden_width, 1)
        term = contract_cols(grad_gate, gate_cols) + contract_cols(grad_up, up_cols)
        term = lax.optimization_barrier(term.astype(jnp.bfloat16)).astype(jnp.float32)
        return carry + term, None

    zeros_in = jnp.zeros((tokens.shape[0], D), jnp.float32)
    input_sum, _ = lax.scan(input_block, zeros_in, jnp.arange(N_GX * N_GY, dtype=jnp.int32))
    input_grad = input_sum.astype(jnp.bfloat16)
    gate_grad = contract_rows(tokens, dgate).astype(jnp.bfloat16)
    up_grad = contract_rows(tokens, dupward).astype(jnp.bfloat16)
    down_grad = contract_rows(hidden, out_grad).astype(jnp.bfloat16)
    return (output, input_grad, gate_grad, up_grad, down_grad)
```

```python
import jax
import jax.numpy as jnp
from jax import lax
from jax.experimental import pallas as pl
from jax.experimental.pallas import tpu as pltpu
from jax.sharding import PartitionSpec as P

BF16 = jnp.bfloat16
F32 = jnp.float32
CORES = 2


def dot(left, right):
    return jnp.dot(left, right, preferred_element_type=F32)


def contract_cols(left, right):
    return lax.dot_general(
        left, right, (((1,), (1,)), ((), ())), preferred_element_type=F32
    )


def tile_of(extent):
    for tile in (256, 128):
        if extent % tile == 0:
            return tile
    return extent


def weight_grad_kernel(left_ref, right_ref, out_ref):
    out_ref[...] = lax.dot_general(
        left_ref[...], right_ref[...], (((0,), (0,)), ((), ())), preferred_element_type=F32
    ).astype(BF16)


def weight_grad(left, right):
    rows, height = left.shape
    width = right.shape[1]
    tile = tile_of(height)
    return pl.pallas_call(
        weight_grad_kernel,
        out_shape=jax.ShapeDtypeStruct((height, width), BF16),
        grid=(height // tile,),
        in_specs=[
            pl.BlockSpec((rows, tile), lambda i: (0, i)),
            pl.BlockSpec((rows, width), lambda i: (0, 0)),
        ],
        out_specs=pl.BlockSpec((tile, width), lambda i: (i, 0)),
        compiler_params=pltpu.CompilerParams(vmem_limit_bytes=24 * 2**20),
        cost_estimate=pl.CostEstimate(
            flops=2 * rows * height * width,
            bytes_accessed=2 * (height * width + rows * (height + width)),
            transcendentals=0,
        ),
    )(left, right)


def shift(x, axis, step):
    n = lax.axis_size(axis)
    return lax.ppermute(x, axis, [(i, (i + step) % n) for i in range(n)])


def other_core(x):
    n = lax.axis_size("gz")
    return lax.ppermute(x, "gz", [(i, i ^ 1) for i in range(n)])


def shift_chip(x, step):
    n = lax.axis_size("gz")
    chips = n // CORES
    return lax.ppermute(
        x, "gz", [(i, (i // CORES + step) % chips * CORES + i % CORES) for i in range(n)]
    )


def gather_gx(own):
    return [own] + [shift(own, "gx", k) for k in range(1, lax.axis_size("gx"))]


def reduce_gz(part):
    half = part.shape[0] // CORES
    total = part[:half].astype(F32) + other_core(part[half:]).astype(F32)
    sent = total.astype(BF16)
    for k in range(1, lax.axis_size("gz") // CORES):
        total = total + shift_chip(sent, k).astype(F32)
    return total


def join_cores(own):
    return jnp.concatenate([own, other_core(own)], axis=0)


def reduce_terms(terms):
    total = terms[0].astype(F32)
    for k in range(1, len(terms)):
        total = total + shift(terms[k], "gx", -k).astype(F32)
    rows, width = total.shape
    n = lax.axis_size("gy")
    me = lax.axis_index("gy")
    core = lax.rem(lax.axis_index("gz"), CORES)
    piece = rows // n
    total = total.astype(BF16)

    def slot(k):
        return lax.rem(me + k, n) * piece

    mine = lax.dynamic_slice_in_dim(total, slot(0), piece, 0).astype(F32)
    for k in range(1, n):
        mine = mine + shift(lax.dynamic_slice_in_dim(total, slot(k), piece, 0), "gy", k).astype(F32)
    mine = mine.astype(BF16)
    result = jnp.zeros((rows, width), BF16)
    for k in range(n):
        got = mine if k == 0 else shift(mine, "gy", k)
        at = lax.rem(slot(n - k) + core * (rows // CORES), rows)
        result = lax.dynamic_update_slice_in_dim(result, got, at, 0)
    return result


def body(tokens, gate_weight, up_weight, down_weight, out_grad):
    core = lax.rem(lax.axis_index("gz"), CORES)
    rows = tokens.shape[0]

    def own_half_first(x):
        return lax.dynamic_slice_in_dim(
            jnp.concatenate([x, x], axis=0), core * (rows // CORES), rows, 0
        )

    toks = gather_gx(own_half_first(tokens))
    grads = gather_gx(own_half_first(out_grad))
    hiddens, dgates, dups, acts = [], [], [], []
    for tok in toks:
        gate = reduce_gz(dot(tok, gate_weight).astype(BF16))
        upward = reduce_gz(dot(tok, up_weight).astype(BF16))
        sig = jax.nn.sigmoid(gate)
        hiddens.append(join_cores((gate * sig * upward).astype(BF16)))
        acts.append((gate, upward, sig))
    output = reduce_terms([dot(h, down_weight).astype(BF16) for h in hiddens])
    for grad, (gate, upward, sig) in zip(grads, acts):
        dhidden = reduce_gz(contract_cols(grad, down_weight).astype(BF16))
        dgates.append(
            join_cores((dhidden * upward * sig * (1.0 + gate * (1.0 - sig))).astype(BF16))
        )
        dups.append(join_cores((dhidden * gate * sig).astype(BF16)))
    input_grad = reduce_terms(
        [
            (contract_cols(dg, gate_weight) + contract_cols(du, up_weight)).astype(BF16)
            for dg, du in zip(dgates, dups)
        ]
    )
    all_tokens = jnp.concatenate(toks, axis=0)
    down_grad = weight_grad(jnp.concatenate(hiddens, axis=0), jnp.concatenate(grads, axis=0))
    gate_grad = weight_grad(all_tokens, jnp.concatenate(dgates, axis=0))
    up_grad = weight_grad(all_tokens, jnp.concatenate(dups, axis=0))
    return (output, input_grad, gate_grad, up_grad, down_grad)


def solution(mesh):
    return jax.shard_map(
        body,
        mesh=mesh,
        in_specs=(
            P("gx", "gz"),
            P("gz", ("gx", "gy")),
            P("gz", ("gx", "gy")),
            P(("gx", "gy"), "gz"),
            P("gx", "gz"),
        ),
        out_specs=(
            P("gx", "gz"),
            P("gx", "gz"),
            P("gz", ("gx", "gy")),
            P("gz", ("gx", "gy")),
            P(("gx", "gy"), "gz"),
        ),
        check_vma=False,
    )
```

```python
import jax
import jax.numpy as jnp
from jax import lax
from jax.experimental import pallas as pl
from jax.experimental.pallas import tpu as pltpu
from jax.sharding import PartitionSpec as P

BF16 = jnp.bfloat16
F32 = jnp.float32
CORES = 2


def dot(left, right):
    return jnp.dot(left, right, preferred_element_type=F32)


def contract_cols(left, right):
    return lax.dot_general(
        left, right, (((1,), (1,)), ((), ())), preferred_element_type=F32
    )


def tile_of(extent):
    for tile in (256, 128):
        if extent % tile == 0:
            return tile
    return extent


def weight_grad_kernel(left_ref, right_ref, out_ref):
    out_ref[...] = lax.dot_general(
        left_ref[...], right_ref[...], (((0,), (0,)), ((), ())), preferred_element_type=F32
    ).astype(BF16)


def weight_grad(left, right):
    rows, height = left.shape
    width = right.shape[1]
    tile = tile_of(height)
    return pl.pallas_call(
        weight_grad_kernel,
        out_shape=jax.ShapeDtypeStruct((height, width), BF16),
        grid=(height // tile,),
        in_specs=[
            pl.BlockSpec((rows, tile), lambda i: (0, i)),
            pl.BlockSpec((rows, width), lambda i: (0, 0)),
        ],
        out_specs=pl.BlockSpec((tile, width), lambda i: (i, 0)),
        compiler_params=pltpu.CompilerParams(vmem_limit_bytes=24 * 2**20),
        cost_estimate=pl.CostEstimate(
            flops=2 * rows * height * width,
            bytes_accessed=2 * (height * width + rows * (height + width)),
            transcendentals=0,
        ),
    )(left, right)


def shift(x, axis, step):
    n = lax.axis_size(axis)
    return lax.ppermute(x, axis, [(i, (i + step) % n) for i in range(n)])


def other_core(x):
    n = lax.axis_size("gz")
    return lax.ppermute(x, "gz", [(i, i ^ 1) for i in range(n)])


def shift_chip(x, step):
    n = lax.axis_size("gz")
    chips = n // CORES
    return lax.ppermute(
        x, "gz", [(i, (i // CORES + step) % chips * CORES + i % CORES) for i in range(n)]
    )


def after(x, *earlier):
    return lax.optimization_barrier((x,) + earlier)[0]


def gather_gx(own):
    return [own] + [shift(own, "gx", k) for k in range(1, lax.axis_size("gx"))]


def halves(blocks, core):
    half = blocks[0].shape[0] // CORES
    return tuple(
        jnp.concatenate(
            [lax.dynamic_slice_in_dim(x, at * half, half, 0) for x in blocks], axis=0
        )
        for at in (core, 1 - core)
    )


def reduce_gz(multiply, mine, other):
    sent = multiply(other).astype(BF16)
    kept = multiply(after(mine, sent)).astype(BF16)
    total = kept.astype(F32) + other_core(sent).astype(F32)
    sent = total.astype(BF16)
    for k in range(1, lax.axis_size("gz") // CORES):
        total = total + shift_chip(sent, k).astype(F32)
    return total, kept


def block_rows(mine, other, k, n):
    half = mine.shape[0] // n
    return jnp.concatenate([mine[k * half : (k + 1) * half], other[k * half : (k + 1) * half]], axis=0)


def reduce_terms(terms):
    total = terms[0].astype(F32)
    for k in range(1, len(terms)):
        total = total + shift(terms[k], "gx", -k).astype(F32)
    rows, width = total.shape
    n = lax.axis_size("gy")
    me = lax.axis_index("gy")
    core = lax.rem(lax.axis_index("gz"), CORES)
    piece = rows // n
    total = total.astype(BF16)

    def slot(k):
        return lax.rem(me + k, n) * piece

    mine = lax.dynamic_slice_in_dim(total, slot(0), piece, 0).astype(F32)
    for k in range(1, n):
        mine = mine + shift(lax.dynamic_slice_in_dim(total, slot(k), piece, 0), "gy", k).astype(F32)
    mine = mine.astype(BF16)
    result = jnp.zeros((rows, width), BF16)
    for k in range(n):
        got = mine if k == 0 else shift(mine, "gy", k)
        at = lax.rem(slot(n - k) + core * (rows // CORES), rows)
        result = lax.dynamic_update_slice_in_dim(result, got, at, 0)
    return result


def body(tokens, gate_weight, up_weight, down_weight, out_grad):
    core = lax.rem(lax.axis_index("gz"), CORES)
    n = lax.axis_size("gx")

    toks = gather_gx(tokens)
    grads = gather_gx(after(out_grad, *toks[1:]))
    tok_mine, tok_other = halves(toks, core)
    gate, gate_part = reduce_gz(lambda x: dot(x, gate_weight), tok_mine, tok_other)
    tok_next = after(tok_other, gate_part)
    upward, up_part = reduce_gz(lambda x: dot(x, up_weight), tok_mine, tok_next)
    grad_mine, grad_other = halves(grads, core)
    grad_next = after(grad_other, up_part)
    dhidden, _ = reduce_gz(lambda x: contract_cols(x, down_weight), grad_mine, grad_next)

    sig = jax.nn.sigmoid(gate)
    hid_mine = (gate * sig * upward).astype(BF16)
    hid_other = other_core(hid_mine)

    terms = [None] * n
    ahead = ()
    for k in list(range(1, n)) + [0]:
        rows = after(block_rows(hid_mine, hid_other, k, n), *ahead)
        terms[k] = dot(rows, down_weight).astype(BF16)
        ahead = (terms[k],)
    output = reduce_terms(terms)

    dhidden = after(dhidden, *ahead)
    dg_mine = (dhidden * upward * sig * (1.0 + gate * (1.0 - sig))).astype(BF16)
    du_mine = (dhidden * gate * sig).astype(BF16)
    dg_other, du_other = other_core(dg_mine), other_core(du_mine)
    ahead = ()
    for k in list(range(1, n)) + [0]:
        dg = after(block_rows(dg_mine, dg_other, k, n), *ahead)
        du = block_rows(du_mine, du_other, k, n)
        terms[k] = (contract_cols(dg, gate_weight) + contract_cols(du, up_weight)).astype(BF16)
        ahead = (terms[k],)
    input_grad = reduce_terms(terms)

    def join(mine, other):
        return jnp.concatenate([mine, other], axis=0)

    all_tokens = join(tok_mine, tok_other)
    down_grad = weight_grad(join(hid_mine, hid_other), join(grad_mine, grad_other))
    gate_grad = weight_grad(after(all_tokens, *ahead), join(dg_mine, dg_other))
    up_grad = weight_grad(after(all_tokens, *ahead), join(du_mine, du_other))
    return (output, input_grad, gate_grad, up_grad, down_grad)


def solution(mesh):
    return jax.shard_map(
        body,
        mesh=mesh,
        in_specs=(
            P("gx", "gz"),
            P("gz", ("gx", "gy")),
            P("gz", ("gx", "gy")),
            P(("gx", "gy"), "gz"),
            P("gx", "gz"),
        ),
        out_specs=(
            P("gx", "gz"),
            P("gx", "gz"),
            P("gz", ("gx", "gy")),
            P("gz", ("gx", "gy")),
            P(("gx", "gy"), "gz"),
        ),
        check_vma=False,
    )
```

```python
import jax
import jax.numpy as jnp
from jax import lax
from jax.experimental import pallas as pl
from jax.experimental.pallas import tpu as pltpu
from jax.sharding import PartitionSpec as P

BF16 = jnp.bfloat16
F32 = jnp.float32
CORES = 2


def dot(left, right):
    return jnp.dot(left, right, preferred_element_type=F32)


def contract_cols(left, right):
    return lax.dot_general(
        left, right, (((1,), (1,)), ((), ())), preferred_element_type=F32
    )


def tile_of(extent):
    for tile in (256, 128):
        if extent % tile == 0:
            return tile
    return extent


def weight_grad_kernel(left_ref, right_ref, out_ref):
    out_ref[...] = lax.dot_general(
        left_ref[...], right_ref[...], (((0,), (0,)), ((), ())), preferred_element_type=F32
    ).astype(BF16)


def weight_grad(left, right):
    rows, height = left.shape
    width = right.shape[1]
    tile = tile_of(height)
    return pl.pallas_call(
        weight_grad_kernel,
        out_shape=jax.ShapeDtypeStruct((height, width), BF16),
        grid=(height // tile,),
        in_specs=[
            pl.BlockSpec((rows, tile), lambda i: (0, i)),
            pl.BlockSpec((rows, width), lambda i: (0, 0)),
        ],
        out_specs=pl.BlockSpec((tile, width), lambda i: (i, 0)),
        compiler_params=pltpu.CompilerParams(vmem_limit_bytes=24 * 2**20),
        cost_estimate=pl.CostEstimate(
            flops=2 * rows * height * width,
            bytes_accessed=2 * (height * width + rows * (height + width)),
            transcendentals=0,
        ),
    )(left, right)


def shift(x, axis, step):
    n = lax.axis_size(axis)
    return lax.ppermute(x, axis, [(i, (i + step) % n) for i in range(n)])


def other_core(x):
    n = lax.axis_size("gz")
    return lax.ppermute(x, "gz", [(i, i ^ 1) for i in range(n)])


def shift_chip(x, step):
    n = lax.axis_size("gz")
    chips = n // CORES
    return lax.ppermute(
        x, "gz", [(i, (i // CORES + step) % chips * CORES + i % CORES) for i in range(n)]
    )


def after(x, *earlier):
    return lax.optimization_barrier((x,) + earlier)[0]


def gather_gx(own):
    return [own] + [shift(own, "gx", k) for k in range(1, lax.axis_size("gx"))]


def halves(blocks, core):
    half = blocks[0].shape[0] // CORES
    return tuple(
        jnp.concatenate(
            [lax.dynamic_slice_in_dim(x, at * half, half, 0) for x in blocks], axis=0
        )
        for at in (core, 1 - core)
    )


def reduce_gz(multiply, mine, other):
    sent = multiply(other).astype(BF16)
    kept = multiply(after(mine, sent)).astype(BF16)
    total = kept.astype(F32) + other_core(sent).astype(F32)
    sent = total.astype(BF16)
    for k in range(1, lax.axis_size("gz") // CORES):
        total = total + shift_chip(sent, k).astype(F32)
    return total, kept, sent


def block_rows(mine, other, k, n):
    half = mine.shape[0] // n
    return jnp.concatenate([mine[k * half : (k + 1) * half], other[k * half : (k + 1) * half]], axis=0)


def reduce_terms(terms, *earlier):
    total = terms[0].astype(F32)
    for k in range(1, len(terms)):
        total = total + after(shift(terms[k], "gx", -k), *earlier).astype(F32)
    rows, width = total.shape
    n = lax.axis_size("gy")
    me = lax.axis_index("gy")
    core = lax.rem(lax.axis_index("gz"), CORES)
    piece = rows // n
    total = total.astype(BF16)

    def slot(k):
        return lax.rem(me + k, n) * piece

    mine = lax.dynamic_slice_in_dim(total, slot(0), piece, 0).astype(F32)
    for k in range(1, n):
        mine = mine + shift(lax.dynamic_slice_in_dim(total, slot(k), piece, 0), "gy", k).astype(F32)
    mine = mine.astype(BF16)
    result = jnp.zeros((rows, width), BF16)
    for k in range(n):
        got = mine if k == 0 else shift(mine, "gy", k)
        at = lax.rem(slot(n - k) + core * (rows // CORES), rows)
        result = lax.dynamic_update_slice_in_dim(result, got, at, 0)
    return result


def body(tokens, gate_weight, up_weight, down_weight, out_grad):
    core = lax.rem(lax.axis_index("gz"), CORES)
    n = lax.axis_size("gx")

    toks = gather_gx(tokens)
    grads = gather_gx(after(out_grad, *toks[1:]))
    tok_mine, tok_other = halves(toks, core)
    gate, gate_part, _ = reduce_gz(lambda x: dot(x, gate_weight), tok_mine, tok_other)
    tok_next = after(tok_other, gate_part)
    upward, _, up_sent = reduce_gz(lambda x: dot(x, up_weight), tok_mine, tok_next)
    grads = [after(x, up_sent) for x in grads]
    grad_mine, grad_other = halves(grads, core)
    dhidden, _, _ = reduce_gz(lambda x: contract_cols(x, down_weight), grad_mine, grad_other)

    sig = jax.nn.sigmoid(gate)
    hid_mine = (gate * sig * upward).astype(BF16)
    hid_other = other_core(hid_mine)

    terms = [None] * n
    ahead = ()
    for k in list(range(1, n)) + [0]:
        rows = after(block_rows(hid_mine, hid_other, k, n), *ahead)
        terms[k] = dot(rows, down_weight).astype(BF16)
        ahead = (terms[k],)
    out_terms = list(terms)

    dhidden = after(dhidden, *ahead)
    dg_mine = (dhidden * upward * sig * (1.0 + gate * (1.0 - sig))).astype(BF16)
    du_mine = (dhidden * gate * sig).astype(BF16)
    dg_other, du_other = other_core(dg_mine), other_core(du_mine)
    ahead = ()
    for k in list(range(1, n)) + [0]:
        dg = after(block_rows(dg_mine, dg_other, k, n), *ahead)
        du = block_rows(du_mine, du_other, k, n)
        terms[k] = (contract_cols(dg, gate_weight) + contract_cols(du, up_weight)).astype(BF16)
        ahead = (terms[k],)
    output = reduce_terms(out_terms, *ahead)
    input_grad = reduce_terms(terms)

    def join(mine, other):
        return jnp.concatenate([mine, other], axis=0)

    all_tokens = join(tok_mine, tok_other)
    down_grad = weight_grad(join(hid_mine, hid_other), join(grad_mine, grad_other))
    gate_grad = weight_grad(after(all_tokens, *ahead), join(dg_mine, dg_other))
    up_grad = weight_grad(after(all_tokens, *ahead), join(du_mine, du_other))
    return (output, input_grad, gate_grad, up_grad, down_grad)


def solution(mesh):
    return jax.shard_map(
        body,
        mesh=mesh,
        in_specs=(
            P("gx", "gz"),
            P("gz", ("gx", "gy")),
            P("gz", ("gx", "gy")),
            P(("gx", "gy"), "gz"),
            P("gx", "gz"),
        ),
        out_specs=(
            P("gx", "gz"),
            P("gx", "gz"),
            P("gz", ("gx", "gy")),
            P("gz", ("gx", "gy")),
            P(("gx", "gy"), "gz"),
        ),
        check_vma=False,
    )
```

```python
import jax
import jax.numpy as jnp
from jax import lax
from jax.experimental import pallas as pl
from jax.experimental.pallas import tpu as pltpu
from jax.sharding import PartitionSpec as P

BF16 = jnp.bfloat16
F32 = jnp.float32
CORES = 2


def dot(left, right):
    return jnp.dot(left, right, preferred_element_type=F32)


def contract_cols(left, right):
    return lax.dot_general(
        left, right, (((1,), (1,)), ((), ())), preferred_element_type=F32
    )


def tile_of(extent):
    for tile in (256, 128):
        if extent % tile == 0:
            return tile
    return extent


def weight_grad_kernel(left_ref, right_ref, out_ref):
    out_ref[...] = lax.dot_general(
        left_ref[...], right_ref[...], (((0,), (0,)), ((), ())), preferred_element_type=F32
    ).astype(BF16)


def weight_grad(left, right):
    rows, height = left.shape
    width = right.shape[1]
    tile = tile_of(height)
    return pl.pallas_call(
        weight_grad_kernel,
        out_shape=jax.ShapeDtypeStruct((height, width), BF16),
        grid=(height // tile,),
        in_specs=[
            pl.BlockSpec((rows, tile), lambda i: (0, i)),
            pl.BlockSpec((rows, width), lambda i: (0, 0)),
        ],
        out_specs=pl.BlockSpec((tile, width), lambda i: (i, 0)),
        compiler_params=pltpu.CompilerParams(vmem_limit_bytes=24 * 2**20),
        cost_estimate=pl.CostEstimate(
            flops=2 * rows * height * width,
            bytes_accessed=2 * (height * width + rows * (height + width)),
            transcendentals=0,
        ),
    )(left, right)


def shift(x, axis, step):
    n = lax.axis_size(axis)
    return lax.ppermute(x, axis, [(i, (i + step) % n) for i in range(n)])


def other_core(x):
    n = lax.axis_size("gz")
    return lax.ppermute(x, "gz", [(i, i ^ 1) for i in range(n)])


def shift_chip(x, step):
    n = lax.axis_size("gz")
    chips = n // CORES
    return lax.ppermute(
        x, "gz", [(i, (i // CORES + step) % chips * CORES + i % CORES) for i in range(n)]
    )


def after(x, *earlier):
    return lax.optimization_barrier((x,) + earlier)[0]


def gather_gx(own):
    return [own] + [shift(own, "gx", k) for k in range(1, lax.axis_size("gx"))]


def halves(blocks, core):
    half = blocks[0].shape[0] // CORES
    return tuple(
        jnp.concatenate(
            [lax.dynamic_slice_in_dim(x, at * half, half, 0) for x in blocks], axis=0
        )
        for at in (core, 1 - core)
    )


def reduce_gz(multiply, mine, other):
    sent = multiply(other).astype(BF16)
    kept = multiply(after(mine, sent)).astype(BF16)
    total = kept.astype(F32) + other_core(sent).astype(F32)
    sent = total.astype(BF16)
    for k in range(1, lax.axis_size("gz") // CORES):
        total = total + shift_chip(sent, k).astype(F32)
    return total, kept, sent


def block_rows(mine, other, k, n):
    half = mine.shape[0] // n
    return jnp.concatenate([mine[k * half : (k + 1) * half], other[k * half : (k + 1) * half]], axis=0)


def reduce_terms(terms, *earlier):
    total = terms[0].astype(F32)
    for k in range(1, len(terms)):
        total = total + after(shift(terms[k], "gx", -k), *earlier).astype(F32)
    rows = total.shape[0]
    n = lax.axis_size("gy")
    me = lax.axis_index("gy")
    core = lax.rem(lax.axis_index("gz"), CORES)
    bits = [1 << j for j in range(n.bit_length() - 1)]
    sides = [lax.rem(me // bit, 2) for bit in bits]

    def swap(x, bit):
        return lax.ppermute(x, "gy", [(i, i ^ bit) for i in range(n)])

    for bit, side in zip(bits, sides):
        half = total.shape[0] // 2
        total_sent = total.astype(BF16)
        kept = lax.dynamic_slice_in_dim(total_sent, side * half, half, 0)
        sent = lax.dynamic_slice_in_dim(total_sent, (1 - side) * half, half, 0)
        total = kept.astype(F32) + swap(sent, bit).astype(F32)
    result = total.astype(BF16)
    for bit, side in zip(reversed(bits), reversed(sides)):
        got = swap(result, bit)
        first = jnp.where(side == 0, result, got)
        last = jnp.where(side == 0, got, result)
        result = jnp.concatenate([first, last], axis=0)
    return lax.dynamic_slice_in_dim(
        jnp.concatenate([result, result], axis=0), core * (rows // CORES), rows, 0
    )


def body(tokens, gate_weight, up_weight, down_weight, out_grad):
    core = lax.rem(lax.axis_index("gz"), CORES)
    n = lax.axis_size("gx")

    toks = gather_gx(tokens)
    grads = gather_gx(after(out_grad, *toks[1:]))
    tok_mine, tok_other = halves(toks, core)
    gate, gate_part, _ = reduce_gz(lambda x: dot(x, gate_weight), tok_mine, tok_other)
    tok_next = after(tok_other, gate_part)
    upward, _, up_sent = reduce_gz(lambda x: dot(x, up_weight), tok_mine, tok_next)
    grads = [after(x, up_sent) for x in grads]
    grad_mine, grad_other = halves(grads, core)
    dhidden, _, _ = reduce_gz(lambda x: contract_cols(x, down_weight), grad_mine, grad_other)

    sig = jax.nn.sigmoid(gate)
    hid_mine = (gate * sig * upward).astype(BF16)
    hid_other = other_core(hid_mine)

    terms = [None] * n
    ahead = ()
    for k in list(range(1, n)) + [0]:
        rows = after(block_rows(hid_mine, hid_other, k, n), *ahead)
        terms[k] = dot(rows, down_weight).astype(BF16)
        ahead = (terms[k],)
    out_terms = list(terms)

    down_grad = weight_grad(
        jnp.concatenate([hid_mine, hid_other], axis=0),
        jnp.concatenate([grad_mine, grad_other], axis=0),
    )
    dhidden = after(dhidden, down_grad, *ahead)
    dg_mine = (dhidden * upward * sig * (1.0 + gate * (1.0 - sig))).astype(BF16)
    du_mine = (dhidden * gate * sig).astype(BF16)
    dg_other, du_other = other_core(dg_mine), other_core(du_mine)
    ahead = ()
    for k in list(range(1, n)) + [0]:
        dg = after(block_rows(dg_mine, dg_other, k, n), *ahead)
        du = block_rows(du_mine, du_other, k, n)
        terms[k] = (contract_cols(dg, gate_weight) + contract_cols(du, up_weight)).astype(BF16)
        ahead = (terms[k],)
    output = reduce_terms(out_terms, *ahead)
    input_grad = reduce_terms(terms)

    def join(mine, other):
        return jnp.concatenate([mine, other], axis=0)

    all_tokens = join(tok_mine, tok_other)
    gate_grad = weight_grad(after(all_tokens, *ahead), join(dg_mine, dg_other))
    up_grad = weight_grad(after(all_tokens, *ahead), join(du_mine, du_other))
    return (output, input_grad, gate_grad, up_grad, down_grad)


def solution(mesh):
    return jax.shard_map(
        body,
        mesh=mesh,
        in_specs=(
            P("gx", "gz"),
            P("gz", ("gx", "gy")),
            P("gz", ("gx", "gy")),
            P(("gx", "gy"), "gz"),
            P("gx", "gz"),
        ),
        out_specs=(
            P("gx", "gz"),
            P("gx", "gz"),
            P("gz", ("gx", "gy")),
            P("gz", ("gx", "gy")),
            P(("gx", "gy"), "gz"),
        ),
        check_vma=False,
    )
```
